1024 devices in a mesh: row: 8 (over x), col: 16 (over y, core), layer: 8 (over z).
Axes of the slice: x: 8, y: 8, z: 8, core: 2. Of those that a mesh axis runs over, the one named last changes fastest.
Arguments:
- h_blocks: float32 [2048, 20, 64, 64], P(('row', 'col', 'layer')), may hold values from -0.17 to 0.17
- h_cols: int32 [2048, 20], P(('row', 'col', 'layer')), may hold values from 0 to 2047, as said below
- z_blocks: float32 [2048, 12, 64, 64], P(('row', 'col', 'layer')), may hold values from -1.1 to 1.1
- z_cols: int32 [2048, 12], P(('row', 'col', 'layer')), may hold values from 0 to 2047, as said below
- out_cols: int32 [2048, 16], P(('row', 'col', 'layer')), may hold values from 0 to 2047, as said below
Outputs:
- orthogonal: float32 [2048, 16, 64, 64], P(('row', 'col', 'layer'))
The draws below stay inside these ranges and needn't reach their ends.
Inputs may be any that keep to these rules, and one draw needn't show every extreme that they name: `h_cols`: row i lists 20 distinct block columns (i + s) mod 2048 with s from -10 to 10, in no particular order; s = 0, -10 and 10 are always among them. `z_cols`: row i lists 12 distinct block columns (i + s) mod 2048 with s from 0 to 12, in no particular order; s = 0 and 12 are always among them. `out_cols`: row a lists 16 distinct block columns (a + s) mod 2048 with s from -10 to 10, in no particular order; s = 0, -10 and 10 are always among them.
All inputs are finite; a program needn't handle non-finite values.
Results may differ from the reference program's by a relative error of at most 0.0003.
Values sent between devices are 32-bit elements; how exact they have to be, the bound alone decides.
No kernel may reach another device: no remote copies, remote signals or barrier semaphores. Data moves between devices by JAX's collectives and lax.ppermute only.
A program may use at most 64 MiB of HBM per device.

```python
import jax
import jax.numpy as jnp
from jax import lax

B = 64
NH = 20
NZ = 12
NO = 16
HS = 10
ZS = 13
NB = 2048


def shuffled_offsets(key, count_rows, forced, pool, chosen_count):
    pool_array = jnp.array(pool, dtype=jnp.int32)
    pool_size = len(pool)
    scores = jax.random.randint(key, (count_rows, pool_size), 0, 1 << 20) * 64 + jnp.arange(pool_size, dtype=jnp.int32)
    order = jnp.argsort(scores, axis=1)
    chosen = pool_array[order[:, :chosen_count]]
    forced_array = jnp.broadcast_to(jnp.array(forced, dtype=jnp.int32), (count_rows, len(forced)))
    joined = jnp.concatenate([forced_array, chosen], axis=1)
    total_width = joined.shape[1]
    second = jax.random.fold_in(key, 7)
    scores_two = jax.random.randint(second, (count_rows, total_width), 0, 1 << 20) * 64 + jnp.arange(total_width, dtype=jnp.int32)
    order_two = jnp.argsort(scores_two, axis=1)
    return jnp.take_along_axis(joined, order_two, axis=1)


def centred_pool():
    return [s for s in range(-HS + 1, HS) if s != 0]


def draw_h_cols(key, part):
    offsets = shuffled_offsets(jax.random.fold_in(key, 11), NB, [0, -HS, HS], centred_pool(), NH - 3)
    return (jnp.arange(NB, dtype=jnp.int32)[:, None] + offsets) % NB


def draw_z_cols(key, part):
    offsets = shuffled_offsets(jax.random.fold_in(key, 12), NB, [0, ZS - 1], list(range(1, ZS - 1)), NZ - 2)
    return (jnp.arange(NB, dtype=jnp.int32)[:, None] + offsets) % NB


def draw_out_cols(key, part):
    offsets = shuffled_offsets(jax.random.fold_in(key, 13), NB, [0, -HS, HS], centred_pool(), NO - 3)
    return (jnp.arange(NB, dtype=jnp.int32)[:, None] + offsets) % NB


def levels(rng, dims, pieces, smallest, top_value):
    factor_of, own = 1.0, jax.random.fold_in(rng, 6)
    for axis_at, parts in pieces:
        steps = jnp.exp(jax.random.uniform(jax.random.fold_in(own, axis_at), (parts,), jnp.float32, smallest / len(pieces), top_value / len(pieces)))
        factor_of = factor_of * jnp.repeat(steps, dims[axis_at] // parts).reshape([-1 if axis == axis_at else 1 for axis in range(len(dims))])
    return factor_of


def bell_draw(stream_key, dims, deviation, reach, split=(), kind=jnp.bfloat16):
    entries = jax.random.normal(stream_key, dims, jnp.float32) * deviation
    if len(split) > 0:
        entries = levels(stream_key, dims, split, -0.22, 0.18) * entries
    return jnp.clip(entries, min=-reach, max=reach).astype(kind)


def setup_inputs(seed: int = 0) -> dict:
    splits = jax.random.split(jax.random.key(seed), 6)
    h_blocks = bell_draw(splits[0], (NB, NH, B, B), 0.028, 0.17, ((0, 1024),), jnp.float32)
    h_cols = draw_h_cols(jax.random.fold_in(splits[5], 71), 0)
    z_blocks = bell_draw(splits[2], (NB, NZ, B, B), 0.19, 1.1, ((0, 1024),), jnp.float32)
    z_cols = draw_z_cols(jax.random.fold_in(splits[5], 71), 0)
    out_cols = draw_out_cols(jax.random.fold_in(splits[5], 71), 0)
    return dict(h_blocks=h_blocks, h_cols=h_cols, z_blocks=z_blocks, z_cols=z_cols, out_cols=out_cols)


EXACT = lax.Precision.HIGHEST


def reference(h_blocks, h_cols, z_blocks, z_cols, out_cols):
    block_size = h_blocks.shape[2]
    width = 2 * HS + 1
    band = 2 * HS + ZS

    def advance(pending, position):
        row_id = position % NB
        h_list = h_cols[row_id]
        h_shift = (h_list - row_id + HS) % NB - HS
        z_rows = z_blocks[h_list]
        z_shift = (z_cols[h_list] - h_list[:, None]) % NB
        products = jnp.einsum('jpk,jmkq->jmpq', h_blocks[row_id], z_rows, precision=EXACT)
        w_band = jnp.zeros((band, block_size, block_size), jnp.float32)
        w_band = w_band.at[h_shift[:, None] + z_shift + HS].add(products)
        own_shift = (z_cols[row_id] - row_id) % NB
        picked = w_band[own_shift[:, None] + jnp.arange(width, dtype=jnp.int32)]
        terms = jnp.einsum('mkp,mokq->mopq', z_blocks[row_id], picked, precision=EXACT)
        pending = pending.at[own_shift].add(terms)
        finished = pending[0]
        pending = jnp.concatenate([pending[1:], jnp.zeros((1, width, block_size, block_size), jnp.float32)], axis=0)
        wanted = (out_cols[row_id] - row_id + HS) % NB
        return pending, finished[wanted]

    start = jnp.zeros((ZS, width, block_size, block_size), jnp.float32)
    _, emitted = lax.scan(advance, start, jnp.arange(-(ZS - 1), NB, dtype=jnp.int32))
    return emitted[ZS - 1:]
```

```python
import functools

import jax
import jax.numpy as jnp
from jax import lax
from jax.experimental import pallas as pl
from jax.experimental.pallas import tpu as pltpu
from jax.sharding import PartitionSpec as P

NH = 20
NZ = 12
NO = 16
HS = 10
ZS = 13
B = 64
AXES = ("row", "col", "layer")
REACH = 5
LAST = 6
NJ = 2 * (2 * REACH + 1)
NC = NJ + ZS - 1
NA = 2 * (LAST + 1)
HALF = NZ // 2 * B
ZROWS = 2 * HALF
SPLIT = False
F32 = jnp.float32
BF16 = jnp.bfloat16

PARAMS = pltpu.CompilerParams(vmem_limit_bytes=48 * 1024 * 1024)


def split(x):
    hi = x.astype(BF16)
    return hi, (x - hi.astype(F32)).astype(BF16)


def shift(x, by):
    size = lax.axis_size(AXES)
    return lax.ppermute(x, AXES, [(i, (i + by) % size) for i in range(size)])


def vmem(count):
    return [pl.BlockSpec(memory_space=pltpu.VMEM)] * count


def smem(count):
    return [pl.BlockSpec(memory_space=pltpu.SMEM)] * count


def pack_kernel(here_ref, cols, z_ref, out_ref, h_off, meta_ref):
    total = here_ref[1]

    def offsets(at, count, low):
        rows = lax.broadcasted_iota(jnp.int32, (2, count), 0) + here_ref[0]
        away = cols[:, at : at + count] - rows
        away = jnp.where(away < low, away + total, away)
        return jnp.where(away >= low + total, away - total, away)

    h_off[...] = offsets(0, NH, -HS)
    meta_ref[...] = jnp.zeros_like(meta_ref)
    meta_ref[0:2, 0:NZ] = offsets(NH, NZ, 0)
    meta_ref[2:4, 0:NO] = offsets(NH + NZ, NO, -HS) + HS
    out_ref[ZROWS:, :] = meta_ref[...].astype(F32)
    for t in range(NZ):
        out_ref[t * B : (t + 1) * B, :] = z_ref[t].T


def pack(here, cols, z_pairs):
    return pl.pallas_call(
        pack_kernel,
        out_shape=(
            jax.ShapeDtypeStruct((ZROWS + 8, 2 * B), F32),
            jax.ShapeDtypeStruct((2, NH), jnp.int32),
            jax.ShapeDtypeStruct((8, 2 * B), jnp.int32),
        ),
        in_specs=smem(1) + vmem(2),
        out_specs=tuple(vmem(3)),
        compiler_params=PARAMS,
        name="pack",
    )(here, cols, z_pairs)


def prep_kernel(h_off, meta, h_ref, z_ref, hh_ref, hl_ref, zz_ref, stack):
    stack[...] = jnp.zeros_like(stack)
    for r in range(2):
        for k in range(NH):
            stack[h_off[r, k] + (HS + r), r * B : (r + 1) * B, :] = h_ref[r, k]
    for e in range(NJ):
        hi, lo = split(stack[e].T)
        hh_ref[e] = hi
        hl_ref[e] = lo
    stack[0:NA] = jnp.zeros((NA,) + stack.shape[1:], F32)
    for r in range(2):
        for m in range(NZ):
            stack[meta[r, m] + r, r * B : (r + 1) * B, :] = z_ref[r, m]
    for a in range(NA):
        hi, lo = split(stack[a].T)
        zz_ref[a, 0:B, 0 : 2 * B] = hi
        zz_ref[a, 0:B, 2 * B :] = hi
        zz_ref[a, B:, 0 : 2 * B] = lo
        zz_ref[a, B:, 2 * B :] = jnp.zeros_like(lo)


def prep(h_off, meta, h_blocks, z_blocks):
    return pl.pallas_call(
        prep_kernel,
        out_shape=(
            jax.ShapeDtypeStruct((NJ, B, 2 * B), BF16),
            jax.ShapeDtypeStruct((NJ, B, 2 * B), BF16),
            jax.ShapeDtypeStruct((NA, 2 * B, 4 * B), BF16),
        ),
        in_specs=smem(2) + vmem(2),
        out_specs=tuple(vmem(3)),
        scratch_shapes=[pltpu.VMEM((NJ, 2 * B, B), F32)],
        compiler_params=PARAMS,
        name="prep",
    )(h_off, meta, h_blocks, z_blocks)


def add_rows(d, meta, x_ref, hh_ref, hl_ref, w_ref):
    for r in range(2):
        e = 2 * (d + REACH) + r
        hi, lo = split(x_ref[r * HALF : (r + 1) * HALF, :])
        hh, hl = hh_ref[e], hl_ref[e]
        none = jnp.zeros_like(hh)
        top = jnp.concatenate([hh, none], axis=1)
        low = jnp.concatenate([none, hh], axis=1)
        main = jnp.concatenate([top, low, top, low], axis=0)
        rest = jnp.concatenate(
            [jnp.concatenate([hl, none], axis=1), jnp.concatenate([none, hl], axis=1)], axis=0
        )
        products = jnp.dot(
            jnp.concatenate([hi, lo], axis=1), main, preferred_element_type=F32
        ) + jnp.dot(hi, rest, preferred_element_type=F32)
        for m in range(NZ):
            at = meta[r, m] + e
            part = products[m // 2 * B : (m // 2 + 1) * B, m % 2 * 2 * B : (m % 2 + 1) * 2 * B]
            w_ref[at] = w_ref[at] + part


def gather_kernel(ds, first, last, *refs):
    n = len(ds)
    metas, xs = refs[:n], refs[n : 2 * n]
    hh_ref, hl_ref = refs[2 * n : 2 * n + 2]
    rest = list(refs[2 * n + 2 :])
    if last:
        w_in, ww_ref, w_ref = rest
        w_ref[...] = w_in[...]
    elif first:
        (w_ref,) = rest
        w_ref[...] = jnp.zeros_like(w_ref)
    else:
        w_in, w_ref = rest
        w_ref[...] = w_in[...]
    for d, meta, x_ref in zip(ds, metas, xs):
        add_rows(d, meta, x_ref, hh_ref, hl_ref, w_ref)
    if last:
        for f in range(NC):
            hi, lo = split(w_ref[f])
            ww_ref[f, :, 0 : 2 * B] = hi
            ww_ref[f, :, 2 * B :] = lo


def gather(ds, metas, xs, hh, hl, w, last):
    first = w is None
    acc = (NC, B, 2 * B)
    return pl.pallas_call(
        functools.partial(gather_kernel, ds, first, last),
        out_shape=jax.ShapeDtypeStruct((NC, B, 4 * B), BF16)
        if last
        else jax.ShapeDtypeStruct(acc, F32),
        in_specs=smem(len(ds)) + vmem(len(ds) + 2 + (not first)),
        out_specs=pl.BlockSpec(memory_space=pltpu.VMEM),
        scratch_shapes=[pltpu.VMEM(acc, F32)] if last else [],
        compiler_params=PARAMS,
        name="gather_last" if last else "gather",
    )(*metas, *xs, hh, hl, *([] if first else [w]))


def spread_kernel(jobs, *refs):
    ks = sorted({k for k, _ in jobs})
    metas = dict(zip(ks, refs))
    zz_ref, ww_ref = refs[len(ks) : len(ks) + 2]
    outs, picked = refs[len(ks) + 2 : -1], refs[-1]
    for slot, ((k, ra), out) in enumerate(zip(jobs, outs)):
        a = 2 * k + ra
        for o in range(NO):
            picked[slot % 2, o * B : (o + 1) * B, :] = ww_ref[metas[k][2 + ra, o] + a]
        both = lax.dot_general(
            zz_ref[a],
            picked[slot % 2],
            (((1,), (1,)), ((), ())),
            preferred_element_type=F32,
        )
        out[...] = both[0:B] + both[B:]


def spread(jobs, metas, zz, ww):
    ks = sorted({k for k, _ in jobs})
    half = jax.ShapeDtypeStruct((B, NO * B), F32)
    return pl.pallas_call(
        functools.partial(spread_kernel, jobs),
        out_shape=(half,) * len(jobs),
        in_specs=smem(len(ks)) + vmem(2),
        out_specs=tuple(vmem(len(jobs))),
        scratch_shapes=[pltpu.VMEM((2, NO * B, 4 * B), BF16)],
        compiler_params=PARAMS,
        name="spread",
    )(*(metas[k] for k in ks), zz, ww)


def unpack_kernel(*refs):
    out_ref = refs[-1]
    for ra in range(2):
        total = refs[3 * ra][...] + refs[3 * ra + 1][...] + refs[3 * ra + 2][...]
        for o in range(NO):
            out_ref[ra, o] = total[:, o * B : (o + 1) * B]


def unpack(*parts):
    return pl.pallas_call(
        unpack_kernel,
        out_shape=jax.ShapeDtypeStruct((2, NO, B, B), F32),
        in_specs=vmem(6),
        out_specs=pl.BlockSpec(memory_space=pltpu.VMEM),
        compiler_params=PARAMS,
        name="unpack",
    )(*parts)


def local(h_blocks, h_cols, z_blocks, z_cols, out_cols):
    here = jnp.stack([lax.axis_index(AXES) * 2, jnp.int32(2 * lax.axis_size(AXES))])
    cols = jnp.concatenate([h_cols, z_cols, out_cols], axis=1)
    own, h_off, meta = pack(here, cols, z_blocks.reshape(NZ, 2 * B, B))
    up = {0: own}
    down = {0: own}
    for d in range(1, REACH):
        up[d] = shift(up[d - 1], -1)
        down[d] = shift(down[d - 1], 1)
    metas = {0: meta}

    def note(d):
        metas[d] = up[d][ZROWS:].astype(jnp.int32)
        metas[-d] = down[d][ZROWS:].astype(jnp.int32)

    for d in range(1, REACH):
        note(d)
    hh, hl, zz = prep(h_off, meta, h_blocks, z_blocks)

    def step(ds, w, last=False):
        xs = [up[d] if d >= 0 else down[-d] for d in ds]
        return gather(ds, [metas[d] for d in ds], xs, hh, hl, w, last)

    w = step((0,), None)
    w = step((1, -1), w)
    w = step((2, -2), w)
    w = step((3, -3), w)
    far_up, far_down, w = lax.optimization_barrier((up[8 - REACH], down[8 - REACH], w))
    up[REACH] = shift(far_down, -8)
    down[REACH] = shift(far_up, 8)
    note(REACH)
    w = step((4, -4), w)
    ww = step((5, -5), w, last=True)

    p40, p41, p51, p50 = spread(((4, 0), (4, 1), (5, 1), (5, 0)), metas, zz, ww)
    head = jnp.pad(up[REACH][ZROWS:], ((0, 0), (0, (NO - 2) * B)))
    back0 = shift(jnp.concatenate([p40, head], axis=0), -1)
    metas[LAST] = back0[B:, 0 : 2 * B].astype(jnp.int32)
    p31, p30, p20, p21, p11, p10, p00, p01 = spread(
        ((3, 1), (3, 0), (2, 0), (2, 1), (1, 1), (1, 0), (0, 0), (0, 1)), metas, zz, ww
    )
    p61, p60 = spread(((6, 1), (6, 0)), metas, zz, ww)
    if SPLIT:
        ahead1 = shift(p41, 1)
        back1 = shift(p51, -1)
        ahead0 = shift(p30, 1)
        ahead1 = shift(ahead1 + p31, 1)
        back0 = shift(back0[0:B] + p50, -1)
        back1 = shift(back1 + p61, LAST)
        ahead0 = shift(ahead0 + p20, 1)
        ahead1 = shift(ahead1 + p21, 1)
        back0 = shift(back0 + p60, LAST)
        ahead0 = shift(ahead0 + p10, 1)
        ahead1 = shift(ahead1 + p11, 1)
    else:
        ahead1 = shift(p41, 1)
        ahead = shift(jnp.concatenate([p30, p31 + ahead1]), 1)
        back = shift(jnp.concatenate([p50 + back0[0:B], p51]), -1)
        ahead = shift(ahead + jnp.concatenate([p20, p21]), 1)
        back = shift(back + jnp.concatenate([p60, p61]), LAST)
        ahead = shift(ahead + jnp.concatenate([p10, p11]), 1)
        ahead0, ahead1 = ahead[0:B], ahead[B:]
        back0, back1 = back[0:B], back[B:]
    return unpack(p00, ahead0, back0, p01, ahead1, back1)


def solution(mesh):
    rows = P(AXES, None)
    blocks = P(AXES, None, None, None)
    return jax.shard_map(
        local,
        mesh=mesh,
        in_specs=(blocks, rows, blocks, rows, rows),
        out_specs=blocks,
        check_vma=False,
    )
```

```python
import functools

import jax
import jax.numpy as jnp
from jax import lax
from jax.experimental import pallas as pl
from jax.experimental.pallas import tpu as pltpu
from jax.sharding import PartitionSpec as P

NH = 20
NZ = 12
NO = 16
HS = 10
ZS = 13
B = 64
AXES = ("row", "col", "layer")
REACH = 5
LAST = 6
NJ = 2 * (2 * REACH + 1)
NC = NJ + ZS - 1
NA = 2 * (LAST + 1)
HALF = NZ // 2 * B
ZROWS = 2 * HALF
F32 = jnp.float32
BF16 = jnp.bfloat16

PARAMS = pltpu.CompilerParams(vmem_limit_bytes=48 * 1024 * 1024)


def split(x):
    hi = x.astype(BF16)
    return hi, (x - hi.astype(F32)).astype(BF16)


def shift(x, by):
    size = lax.axis_size(AXES)
    return lax.ppermute(x, AXES, [(i, (i + by) % size) for i in range(size)])


def vmem(count):
    return [pl.BlockSpec(memory_space=pltpu.VMEM)] * count


def smem(count):
    return [pl.BlockSpec(memory_space=pltpu.SMEM)] * count


def pack_kernel(here_ref, cols, z_ref, out_ref, h_off, meta_ref):
    total = here_ref[1]

    def offsets(at, count, low):
        rows = lax.broadcasted_iota(jnp.int32, (2, count), 0) + here_ref[0]
        away = cols[:, at : at + count] - rows
        away = jnp.where(away < low, away + total, away)
        return jnp.where(away >= low + total, away - total, away)

    h_off[...] = offsets(0, NH, -HS)
    meta_ref[...] = jnp.zeros_like(meta_ref)
    meta_ref[0:2, 0:NZ] = offsets(NH, NZ, 0)
    meta_ref[2:4, 0:NO] = offsets(NH + NZ, NO, -HS) + HS
    out_ref[ZROWS:, :] = meta_ref[...].astype(F32)
    for t in range(NZ):
        out_ref[t * B : (t + 1) * B, :] = z_ref[t].T


def pack(here, cols, z_pairs):
    return pl.pallas_call(
        pack_kernel,
        out_shape=(
            jax.ShapeDtypeStruct((ZROWS + 8, 2 * B), F32),
            jax.ShapeDtypeStruct((2, NH), jnp.int32),
            jax.ShapeDtypeStruct((8, 2 * B), jnp.int32),
        ),
        in_specs=smem(1) + vmem(2),
        out_specs=tuple(vmem(3)),
        compiler_params=PARAMS,
        name="pack",
    )(here, cols, z_pairs)


def prep_kernel(h_off, meta, h_ref, z_ref, hh_ref, hl_ref, zz_ref, stack):
    stack[...] = jnp.zeros_like(stack)
    for r in range(2):
        for k in range(NH):
            stack[h_off[r, k] + (HS + r), r * B : (r + 1) * B, :] = h_ref[r, k]
    for e in range(NJ):
        hi, lo = split(stack[e].T)
        hh_ref[e] = hi
        hl_ref[e] = lo
    stack[0:NA] = jnp.zeros((NA,) + stack.shape[1:], F32)
    for r in range(2):
        for m in range(NZ):
            stack[meta[r, m] + r, r * B : (r + 1) * B, :] = z_ref[r, m]
    for a in range(NA):
        hi, lo = split(stack[a].T)
        zz_ref[a, 0:B, 0 : 2 * B] = hi
        zz_ref[a, 0:B, 2 * B :] = hi
        zz_ref[a, B:, 0 : 2 * B] = lo
        zz_ref[a, B:, 2 * B :] = jnp.zeros_like(lo)


def prep(h_off, meta, h_blocks, z_blocks):
    return pl.pallas_call(
        prep_kernel,
        out_shape=(
            jax.ShapeDtypeStruct((NJ, B, 2 * B), BF16),
            jax.ShapeDtypeStruct((NJ, B, 2 * B), BF16),
            jax.ShapeDtypeStruct((NA, 2 * B, 4 * B), BF16),
        ),
        in_specs=smem(2) + vmem(2),
        out_specs=tuple(vmem(3)),
        scratch_shapes=[pltpu.VMEM((NJ, 2 * B, B), F32)],
        compiler_params=PARAMS,
        name="prep",
    )(h_off, meta, h_blocks, z_blocks)


def add_rows(d, meta, x_ref, hh_ref, hl_ref, w_ref):
    for r in range(2):
        e = 2 * (d + REACH) + r
        hi, lo = split(x_ref[r * HALF : (r + 1) * HALF, :])
        hh, hl = hh_ref[e], hl_ref[e]
        none = jnp.zeros_like(hh)
        top = jnp.concatenate([hh, none], axis=1)
        low = jnp.concatenate([none, hh], axis=1)
        main = jnp.concatenate([top, low, top, low], axis=0)
        rest = jnp.concatenate(
            [jnp.concatenate([hl, none], axis=1), jnp.concatenate([none, hl], axis=1)], axis=0
        )
        products = jnp.dot(
            jnp.concatenate([hi, lo], axis=1), main, preferred_element_type=F32
        ) + jnp.dot(hi, rest, preferred_element_type=F32)
        for m in range(NZ):
            at = meta[r, m] + e
            part = products[m // 2 * B : (m // 2 + 1) * B, m % 2 * 2 * B : (m % 2 + 1) * 2 * B]
            w_ref[at] = w_ref[at] + part


def gather_kernel(ds, first, last, *refs):
    n = len(ds)
    metas, xs = refs[:n], refs[n : 2 * n]
    hh_ref, hl_ref = refs[2 * n : 2 * n + 2]
    rest = list(refs[2 * n + 2 :])
    if last:
        w_in, ww_ref, w_ref = rest
        w_ref[...] = w_in[...]
    elif first:
        (w_ref,) = rest
        w_ref[...] = jnp.zeros_like(w_ref)
    else:
        w_in, w_ref = rest
        w_ref[...] = w_in[...]
    for d, meta, x_ref in zip(ds, metas, xs):
        add_rows(d, meta, x_ref, hh_ref, hl_ref, w_ref)
    if last:
        for f in range(NC):
            hi, lo = split(w_ref[f])
            ww_ref[f, :, 0 : 2 * B] = hi
            ww_ref[f, :, 2 * B :] = lo


def gather(ds, metas, xs, hh, hl, w, last):
    first = w is None
    acc = (NC, B, 2 * B)
    return pl.pallas_call(
        functools.partial(gather_kernel, ds, first, last),
        out_shape=jax.ShapeDtypeStruct((NC, B, 4 * B), BF16)
        if last
        else jax.ShapeDtypeStruct(acc, F32),
        in_specs=smem(len(ds)) + vmem(len(ds) + 2 + (not first)),
        out_specs=pl.BlockSpec(memory_space=pltpu.VMEM),
        scratch_shapes=[pltpu.VMEM(acc, F32)] if last else [],
        compiler_params=PARAMS,
        name="gather_last" if last else "gather",
    )(*metas, *xs, hh, hl, *([] if first else [w]))


def spread_kernel(jobs, *refs):
    ks = sorted({k for k, _ in jobs})
    metas = dict(zip(ks, refs))
    zz_ref, ww_ref = refs[len(ks) : len(ks) + 2]
    outs, picked = refs[len(ks) + 2 : -1], refs[-1]
    for slot, ((k, ra), out) in enumerate(zip(jobs, outs)):
        a = 2 * k + ra
        for o in range(NO):
            picked[slot % 2, o * B : (o + 1) * B, :] = ww_ref[metas[k][2 + ra, o] + a]
        both = lax.dot_general(
            zz_ref[a],
            picked[slot % 2],
            (((1,), (1,)), ((), ())),
            preferred_element_type=F32,
        )
        out[...] = both[0:B] + both[B:]


def spread(jobs, metas, zz, ww):
    ks = sorted({k for k, _ in jobs})
    half = jax.ShapeDtypeStruct((B, NO * B), F32)
    return pl.pallas_call(
        functools.partial(spread_kernel, jobs),
        out_shape=(half,) * len(jobs),
        in_specs=smem(len(ks)) + vmem(2),
        out_specs=tuple(vmem(len(jobs))),
        scratch_shapes=[pltpu.VMEM((2, NO * B, 4 * B), BF16)],
        compiler_params=PARAMS,
        name="spread",
    )(*(metas[k] for k in ks), zz, ww)


def unpack_kernel(*refs):
    out_ref = refs[-1]
    for ra in range(2):
        total = refs[3 * ra][...] + refs[3 * ra + 1][...] + refs[3 * ra + 2][...]
        for o in range(NO):
            out_ref[ra, o] = total[:, o * B : (o + 1) * B]


def unpack(*parts):
    return pl.pallas_call(
        unpack_kernel,
        out_shape=jax.ShapeDtypeStruct((2, NO, B, B), F32),
        in_specs=vmem(6),
        out_specs=pl.BlockSpec(memory_space=pltpu.VMEM),
        compiler_params=PARAMS,
        name="unpack",
    )(*parts)


def local(h_blocks, h_cols, z_blocks, z_cols, out_cols):
    here = jnp.stack([lax.axis_index(AXES) * 2, jnp.int32(2 * lax.axis_size(AXES))])
    cols = jnp.concatenate([h_cols, z_cols, out_cols], axis=1)
    own, h_off, meta = pack(here, cols, z_blocks.reshape(NZ, 2 * B, B))
    up = {0: own}
    down = {0: own}
    for d in range(1, REACH):
        up[d] = shift(up[d - 1], -1)
        down[d] = shift(down[d - 1], 1)
    metas = {0: meta}
    down[REACH] = shift(up[8 - REACH], 8)
    far = jnp.concatenate(
        [down[8 - REACH][0 : ZROWS + 4], down[8 - LAST][ZROWS : ZROWS + 4]], axis=0
    )
    up[REACH] = shift(far, -8)
    down[REACH], up[REACH] = lax.optimization_barrier((down[REACH], up[REACH]))

    def note(d):
        metas[d] = up[d][ZROWS:].astype(jnp.int32)
        metas[-d] = down[d][ZROWS:].astype(jnp.int32)

    for d in range(1, REACH + 1):
        note(d)
    metas[LAST] = up[REACH][ZROWS + 4 :].astype(jnp.int32)
    hh, hl, zz = prep(h_off, meta, h_blocks, z_blocks)

    def step(ds, w, last=False):
        xs = [up[d] if d >= 0 else down[-d] for d in ds]
        return gather(ds, [metas[d] for d in ds], xs, hh, hl, w, last)

    w = step((0,), None)
    w = step((1, -1), w)
    w = step((2, -2), w)
    w = step((3, -3), w)
    w = step((4, -4), w)
    ww = step((5, -5), w, last=True)

    def parts(*jobs):
        return spread(jobs, metas, zz, ww)

    p50, p51 = parts((5, 0), (5, 1))
    back = shift(jnp.concatenate([p50, p51], axis=0), -1)
    p41, p40 = parts((4, 1), (4, 0))
    ahead1 = shift(p41, 1)
    ahead0 = shift(p40, 1)
    p31, p30, p60, p61, p21, p20, p11, p10, p00, p01 = parts(
        (3, 1), (3, 0), (6, 0), (6, 1), (2, 1), (2, 0), (1, 1), (1, 0), (0, 0), (0, 1)
    )
    ahead1 = shift(ahead1 + p31, 1)
    ahead0 = shift(ahead0 + p30, 1)
    back = shift(back + jnp.concatenate([p60, p61], axis=0), LAST)
    ahead1 = shift(ahead1 + p21, 1)
    ahead0 = shift(ahead0 + p20, 1)
    ahead1 = shift(ahead1 + p11, 1)
    ahead0 = shift(ahead0 + p10, 1)
    back0, back1 = back[0:B], back[B:]
    return unpack(p00, ahead0, back0, p01, ahead1, back1)


def solution(mesh):
    rows = P(AXES, None)
    blocks = P(AXES, None, None, None)
    return jax.shard_map(
        local,
        mesh=mesh,
        in_specs=(blocks, rows, blocks, rows, rows),
        out_specs=blocks,
        check_vma=False,
    )
```

```python
import functools

import jax
import jax.numpy as jnp
from jax import lax
from jax.experimental import pallas as pl
from jax.experimental.pallas import tpu as pltpu
from jax.sharding import PartitionSpec as P

NH = 20
NZ = 12
NO = 16
HS = 10
ZS = 13
B = 64
AXES = ("row", "col", "layer")
REACH = 5
LAST = 6
NJ = 2 * (2 * REACH + 1)
NC = NJ + ZS - 1
NA = 2 * (LAST + 1)
HALF = NZ // 2 * B
ZROWS = 2 * HALF
F32 = jnp.float32
BF16 = jnp.bfloat16

PARAMS = pltpu.CompilerParams(vmem_limit_bytes=48 * 1024 * 1024)


def split(x):
    hi = x.astype(BF16)
    return hi, (x - hi.astype(F32)).astype(BF16)


def shift(x, by):
    size = lax.axis_size(AXES)
    return lax.ppermute(x, AXES, [(i, (i + by) % size) for i in range(size)])


def vmem(count):
    return [pl.BlockSpec(memory_space=pltpu.VMEM)] * count


def smem(count):
    return [pl.BlockSpec(memory_space=pltpu.SMEM)] * count


def pack_kernel(here_ref, cols, z_ref, out_ref, h_off, meta_ref):
    total = here_ref[1]

    def offsets(at, count, low):
        rows = lax.broadcasted_iota(jnp.int32, (2, count), 0) + here_ref[0]
        away = cols[:, at : at + count] - rows
        away = jnp.where(away < low, away + total, away)
        return jnp.where(away >= low + total, away - total, away)

    h_off[...] = offsets(0, NH, -HS)
    meta_ref[...] = jnp.zeros_like(meta_ref)
    meta_ref[0:2, 0:NZ] = offsets(NH, NZ, 0)
    meta_ref[2:4, 0:NO] = offsets(NH + NZ, NO, -HS) + HS
    out_ref[ZROWS:, :] = meta_ref[...].astype(F32)
    for t in range(NZ):
        out_ref[t * B : (t + 1) * B, :] = z_ref[t].T


def pack(here, cols, z_pairs):
    return pl.pallas_call(
        pack_kernel,
        out_shape=(
            jax.ShapeDtypeStruct((ZROWS + 8, 2 * B), F32),
            jax.ShapeDtypeStruct((2, NH), jnp.int32),
            jax.ShapeDtypeStruct((8, 2 * B), jnp.int32),
        ),
        in_specs=smem(1) + vmem(2),
        out_specs=tuple(vmem(3)),
        compiler_params=PARAMS,
        name="pack",
    )(here, cols, z_pairs)


def prep_kernel(h_off, meta, h_ref, z_ref, hh_ref, hl_ref, zz_ref, stack):
    stack[...] = jnp.zeros_like(stack)
    for r in range(2):
        for k in range(NH):
            stack[h_off[r, k] + (HS + r), r * B : (r + 1) * B, :] = h_ref[r, k]
    for e in range(NJ):
        hi, lo = split(stack[e].T)
        hh_ref[e] = hi
        hl_ref[e] = lo
    stack[0:NA] = jnp.zeros((NA,) + stack.shape[1:], F32)
    for r in range(2):
        for m in range(NZ):
            stack[meta[r, m] + r, r * B : (r + 1) * B, :] = z_ref[r, m]
    for a in range(NA):
        hi, lo = split(stack[a].T)
        zz_ref[a, 0:B, 0 : 2 * B] = hi
        zz_ref[a, 0:B, 2 * B :] = hi
        zz_ref[a, B:, 0 : 2 * B] = lo
        zz_ref[a, B:, 2 * B :] = jnp.zeros_like(lo)


def prep(h_off, meta, h_blocks, z_blocks):
    return pl.pallas_call(
        prep_kernel,
        out_shape=(
            jax.ShapeDtypeStruct((NJ, B, 2 * B), BF16),
            jax.ShapeDtypeStruct((NJ, B, 2 * B), BF16),
            jax.ShapeDtypeStruct((NA, 2 * B, 4 * B), BF16),
        ),
        in_specs=smem(2) + vmem(2),
        out_specs=tuple(vmem(3)),
        scratch_shapes=[pltpu.VMEM((NJ, 2 * B, B), F32)],
        compiler_params=PARAMS,
        name="prep",
    )(h_off, meta, h_blocks, z_blocks)


def add_rows(d, meta, x_ref, hh_ref, hl_ref, w_ref):
    for r in range(2):
        e = 2 * (d + REACH) + r
        hi, lo = split(x_ref[r * HALF : (r + 1) * HALF, :])
        hh, hl = hh_ref[e], hl_ref[e]
        none = jnp.zeros_like(hh)
        top = jnp.concatenate([hh, none], axis=1)
        low = jnp.concatenate([none, hh], axis=1)
        main = jnp.concatenate([top, low, top, low], axis=0)
        rest = jnp.concatenate(
            [jnp.concatenate([hl, none], axis=1), jnp.concatenate([none, hl], axis=1)], axis=0
        )
        products = jnp.dot(
            jnp.concatenate([hi, lo], axis=1), main, preferred_element_type=F32
        ) + jnp.dot(hi, rest, preferred_element_type=F32)
        for m in range(NZ):
            at = meta[r, m] + e
            part = products[m // 2 * B : (m // 2 + 1) * B, m % 2 * 2 * B : (m % 2 + 1) * 2 * B]
            w_ref[at] = w_ref[at] + part


def gather_kernel(ds, first, *refs):
    n = len(ds)
    metas, xs = refs[:n], refs[n : 2 * n]
    hh_ref, hl_ref, w_ref = refs[2 * n], refs[2 * n + 1], refs[-1]
    w_ref[...] = jnp.zeros_like(w_ref) if first else refs[-2][...]
    for d, meta, x_ref in zip(ds, metas, xs):
        add_rows(d, meta, x_ref, hh_ref, hl_ref, w_ref)


def gather(ds, metas, xs, hh, hl, w):
    n = len(ds)
    first = w is None
    return pl.pallas_call(
        functools.partial(gather_kernel, ds, first),
        out_shape=jax.ShapeDtypeStruct((NC, B, 2 * B), F32),
        in_specs=smem(n) + vmem(n + 2 + (not first)),
        out_specs=pl.BlockSpec(memory_space=pltpu.VMEM),
        compiler_params=PARAMS,
        name="gather",
    )(*metas, *xs, hh, hl, *([] if first else [w]))


def spread_half(k, ra, meta, zz_ref, ww_ref, picked, out):
    a = 2 * k + ra
    for o in range(NO):
        picked[o * B : (o + 1) * B, :] = ww_ref[meta[2 + ra, o] + a]
    both = lax.dot_general(
        zz_ref[a], picked[...], (((1,), (1,)), ((), ())), preferred_element_type=F32
    )
    out[...] = both[0:B] + both[B:]


def spread_kernel(jobs, *refs):
    ks = sorted({k for k, _ in jobs})
    metas = dict(zip(ks, refs))
    zz_ref, ww_ref = refs[len(ks) : len(ks) + 2]
    outs, picked = refs[len(ks) + 2 : -1], refs[-1]
    for slot, ((k, ra), out) in enumerate(zip(jobs, outs)):
        spread_half(k, ra, metas[k], zz_ref, ww_ref, picked.at[slot % 2], out)


def spread(jobs, metas, zz, ww):
    ks = sorted({k for k, _ in jobs})
    half = jax.ShapeDtypeStruct((B, NO * B), F32)
    return pl.pallas_call(
        functools.partial(spread_kernel, jobs),
        out_shape=(half,) * len(jobs),
        in_specs=smem(len(ks)) + vmem(2),
        out_specs=tuple(vmem(len(jobs))),
        scratch_shapes=[pltpu.VMEM((2, NO * B, 4 * B), BF16)],
        compiler_params=PARAMS,
        name="spread",
    )(*(metas[k] for k in ks), zz, ww)


def finish_kernel(ds, m0, m1, m4, x0, x1, hh_ref, hl_ref, zz_ref, w_in, *refs):
    ww_ref, p5, p41, p40, w_ref, picked = refs
    w_ref[...] = w_in[...]
    for d, meta, x_ref in zip(ds, (m0, m1), (x0, x1)):
        add_rows(d, meta, x_ref, hh_ref, hl_ref, w_ref)
    for f in range(NC):
        hi, lo = split(w_ref[f])
        ww_ref[f, :, 0 : 2 * B] = hi
        ww_ref[f, :, 2 * B :] = lo
    spread_half(5, 0, m0, zz_ref, ww_ref, picked.at[0], p5.at[0:B])
    spread_half(5, 1, m0, zz_ref, ww_ref, picked.at[1], p5.at[B : 2 * B])
    spread_half(4, 1, m4, zz_ref, ww_ref, picked.at[0], p41)
    spread_half(4, 0, m4, zz_ref, ww_ref, picked.at[1], p40)


def finish(ds, metas, xs, hh, hl, zz, w):
    half = jax.ShapeDtypeStruct((B, NO * B), F32)
    return pl.pallas_call(
        functools.partial(finish_kernel, ds),
        out_shape=(
            jax.ShapeDtypeStruct((NC, B, 4 * B), BF16),
            jax.ShapeDtypeStruct((2 * B, NO * B), F32),
            half,
            half,
        ),
        in_specs=smem(3) + vmem(6),
        out_specs=tuple(vmem(4)),
        scratch_shapes=[
            pltpu.VMEM((NC, B, 2 * B), F32),
            pltpu.VMEM((2, NO * B, 4 * B), BF16),
        ],
        compiler_params=PARAMS,
        name="finish",
    )(*metas, *xs, hh, hl, zz, w)


def unpack_kernel(*refs):
    out_ref = refs[-1]
    for ra in range(2):
        total = refs[3 * ra][...] + refs[3 * ra + 1][...] + refs[3 * ra + 2][...]
        for o in range(NO):
            out_ref[ra, o] = total[:, o * B : (o + 1) * B]


def unpack(*parts):
    return pl.pallas_call(
        unpack_kernel,
        out_shape=jax.ShapeDtypeStruct((2, NO, B, B), F32),
        in_specs=vmem(6),
        out_specs=pl.BlockSpec(memory_space=pltpu.VMEM),
        compiler_params=PARAMS,
        name="unpack",
    )(*parts)


def local(h_blocks, h_cols, z_blocks, z_cols, out_cols):
    here = jnp.stack([lax.axis_index(AXES) * 2, jnp.int32(2 * lax.axis_size(AXES))])
    cols = jnp.concatenate([h_cols, z_cols, out_cols], axis=1)
    own, h_off, meta = pack(here, cols, z_blocks.reshape(NZ, 2 * B, B))
    up = {0: own}
    down = {0: own}
    for d in range(1, REACH):
        up[d] = shift(up[d - 1], -1)
        down[d] = shift(down[d - 1], 1)
    metas = {0: meta}
    down[REACH] = shift(up[8 - REACH], 8)
    far = jnp.concatenate(
        [down[8 - REACH][0 : ZROWS + 4], down[8 - LAST][ZROWS : ZROWS + 4]], axis=0
    )
    up[REACH] = shift(far, -8)
    down[REACH], up[REACH] = lax.optimization_barrier((down[REACH], up[REACH]))

    def note(d):
        metas[d] = up[d][ZROWS:].astype(jnp.int32)
        metas[-d] = down[d][ZROWS:].astype(jnp.int32)

    for d in range(1, REACH + 1):
        note(d)
    metas[LAST] = up[REACH][ZROWS + 4 :].astype(jnp.int32)
    hh, hl, zz = prep(h_off, meta, h_blocks, z_blocks)

    def step(ds, w):
        xs = [up[d] if d >= 0 else down[-d] for d in ds]
        return gather(ds, [metas[d] for d in ds], xs, hh, hl, w)

    w = step((0,), None)
    w = step((1, -1), w)
    w = step((2, -2), w)
    w = step((3, -3), w)
    w = step((4, -4), w)
    ww, p5, p41, p40 = finish(
        (REACH, -REACH),
        (metas[REACH], metas[-REACH], metas[4]),
        (up[REACH], down[REACH]),
        hh,
        hl,
        zz,
        w,
    )

    def parts(*jobs):
        return spread(jobs, metas, zz, ww)

    back = shift(p5, -1)
    ahead1 = shift(p41, 1)
    ahead0 = shift(p40, 1)
    p31, p30, p60, p61, p21, p20, p11, p10, p00, p01 = parts(
        (3, 1), (3, 0), (6, 0), (6, 1), (2, 1), (2, 0), (1, 1), (1, 0), (0, 0), (0, 1)
    )
    ahead1 = shift(ahead1 + p31, 1)
    ahead0 = shift(ahead0 + p30, 1)
    back = shift(back + jnp.concatenate([p60, p61], axis=0), LAST)
    ahead1 = shift(ahead1 + p21, 1)
    ahead0 = shift(ahead0 + p20, 1)
    ahead1 = shift(ahead1 + p11, 1)
    ahead0 = shift(ahead0 + p10, 1)
    back0, back1 = back[0:B], back[B:]
    return unpack(p00, ahead0, back0, p01, ahead1, back1)


def solution(mesh):
    rows = P(AXES, None)
    blocks = P(AXES, None, None, None)
    return jax.shard_map(
        local,
        mesh=mesh,
        in_specs=(blocks, rows, blocks, rows, rows),
        out_specs=blocks,
        check_vma=False,
    )
```

```python
import functools

import jax
import jax.numpy as jnp
from jax import lax
from jax.experimental import pallas as pl
from jax.experimental.pallas import tpu as pltpu
from jax.sharding import PartitionSpec as P

NH = 20
NZ = 12
NO = 16
HS = 10
ZS = 13
B = 64
AXES = ("row", "col", "layer")
REACH = 5
LAST = 6
NJ = 2 * (2 * REACH + 1)
NC = NJ + ZS - 1
NA = 2 * (LAST + 1)
HALF = NZ // 2 * B
ZROWS = 2 * HALF
F32 = jnp.float32
BF16 = jnp.bfloat16

PARAMS = pltpu.CompilerParams(vmem_limit_bytes=48 * 1024 * 1024)


def split(x):
    hi = x.astype(BF16)
    return hi, (x - hi.astype(F32)).astype(BF16)


def shift(x, by):
    size = lax.axis_size(AXES)
    return lax.ppermute(x, AXES, [(i, (i + by) % size) for i in range(size)])


def vmem(count):
    return [pl.BlockSpec(memory_space=pltpu.VMEM)] * count


def smem(count):
    return [pl.BlockSpec(memory_space=pltpu.SMEM)] * count


def pack_kernel(here_ref, cols, z_ref, out_ref, h_off, meta_ref):
    total = here_ref[1]

    def offsets(at, count, low):
        rows = lax.broadcasted_iota(jnp.int32, (2, count), 0) + here_ref[0]
        away = cols[:, at : at + count] - rows
        away = jnp.where(away < low, away + total, away)
        return jnp.where(away >= low + total, away - total, away)

    h_off[...] = offsets(0, NH, -HS)
    meta_ref[...] = jnp.zeros_like(meta_ref)
    meta_ref[0:2, 0:NZ] = offsets(NH, NZ, 0)
    meta_ref[2:4, 0:NO] = offsets(NH + NZ, NO, -HS) + HS
    out_ref[ZROWS:, :] = meta_ref[...].astype(F32)
    for t in range(NZ):
        out_ref[t * B : (t + 1) * B, :] = z_ref[t].T


def pack(here, cols, z_pairs):
    return pl.pallas_call(
        pack_kernel,
        out_shape=(
            jax.ShapeDtypeStruct((ZROWS + 8, 2 * B), F32),
            jax.ShapeDtypeStruct((2, NH), jnp.int32),
            jax.ShapeDtypeStruct((8, 2 * B), jnp.int32),
        ),
        in_specs=smem(1) + vmem(2),
        out_specs=tuple(vmem(3)),
        compiler_params=PARAMS,
        name="pack",
    )(here, cols, z_pairs)


def prep_kernel(h_off, meta, h_ref, z_ref, hh_ref, hl_ref, zz_ref, stack):
    stack[...] = jnp.zeros_like(stack)
    for r in range(2):
        for k in range(NH):
            stack[h_off[r, k] + (HS + r), r * B : (r + 1) * B, :] = h_ref[r, k]
    for e in range(NJ):
        hi, lo = split(stack[e].T)
        hh_ref[e] = hi
        hl_ref[e] = lo
    stack[0:NA] = jnp.zeros((NA,) + stack.shape[1:], F32)
    for r in range(2):
        for m in range(NZ):
            stack[meta[r, m] + r, r * B : (r + 1) * B, :] = z_ref[r, m]
    for a in range(NA):
        hi, lo = split(stack[a].T)
        zz_ref[a, 0:B, 0 : 2 * B] = hi
        zz_ref[a, 0:B, 2 * B :] = hi
        zz_ref[a, B:, 0 : 2 * B] = lo
        zz_ref[a, B:, 2 * B :] = jnp.zeros_like(lo)


def prep(h_off, meta, h_blocks, z_blocks):
    return pl.pallas_call(
        prep_kernel,
        out_shape=(
            jax.ShapeDtypeStruct((NJ, B, 2 * B), BF16),
            jax.ShapeDtypeStruct((NJ, B, 2 * B), BF16),
            jax.ShapeDtypeStruct((NA, 2 * B, 4 * B), BF16),
        ),
        in_specs=smem(2) + vmem(2),
        out_specs=tuple(vmem(3)),
        scratch_shapes=[pltpu.VMEM((NJ, 2 * B, B), F32)],
        compiler_params=PARAMS,
        name="prep",
    )(h_off, meta, h_blocks, z_blocks)


def add_rows(d, meta, x_ref, hh_ref, hl_ref, w_ref):
    for r in range(2):
        e = 2 * (d + REACH) + r
        hi, lo = split(x_ref[r * HALF : (r + 1) * HALF, :])
        hh, hl = hh_ref[e], hl_ref[e]
        none = jnp.zeros_like(hh)
        top = jnp.concatenate([hh, none], axis=1)
        low = jnp.concatenate([none, hh], axis=1)
        main = jnp.concatenate([top, low, top, low], axis=0)
        rest = jnp.concatenate(
            [jnp.concatenate([hl, none], axis=1), jnp.concatenate([none, hl], axis=1)], axis=0
        )
        products = jnp.dot(
            jnp.concatenate([hi, lo], axis=1), main, preferred_element_type=F32
        ) + jnp.dot(hi, rest, preferred_element_type=F32)
        for m in range(NZ):
            at = meta[r, m] + e
            part = products[m // 2 * B : (m // 2 + 1) * B, m % 2 * 2 * B : (m % 2 + 1) * 2 * B]
            w_ref[at] = w_ref[at] + part


def gather_kernel(ds, first, *refs):
    n = len(ds)
    metas, xs = refs[:n], refs[n : 2 * n]
    hh_ref, hl_ref, w_ref = refs[2 * n], refs[2 * n + 1], refs[-1]
    w_ref[...] = jnp.zeros_like(w_ref) if first else refs[-2][...]
    for d, meta, x_ref in zip(ds, metas, xs):
        add_rows(d, meta, x_ref, hh_ref, hl_ref, w_ref)


def gather(ds, metas, xs, hh, hl, w):
    n = len(ds)
    first = w is None
    return pl.pallas_call(
        functools.partial(gather_kernel, ds, first),
        out_shape=jax.ShapeDtypeStruct((NC, B, 2 * B), F32),
        in_specs=smem(n) + vmem(n + 2 + (not first)),
        out_specs=pl.BlockSpec(memory_space=pltpu.VMEM),
        compiler_params=PARAMS,
        name="gather",
    )(*metas, *xs, hh, hl, *([] if first else [w]))


def spread_half(k, ra, meta, zz_ref, ww_ref, picked, out):
    a = 2 * k + ra
    for o in range(NO):
        picked[o * B : (o + 1) * B, :] = ww_ref[meta[2 + ra, o] + a]
    both = lax.dot_general(
        zz_ref[a], picked[...], (((1,), (1,)), ((), ())), preferred_element_type=F32
    )
    out[...] = both[0:B] + both[B:]


def spread_kernel(jobs, *refs):
    ks = sorted({k for k, _ in jobs})
    metas = dict(zip(ks, refs))
    zz_ref, ww_ref = refs[len(ks) : len(ks) + 2]
    outs, picked = refs[len(ks) + 2 : -1], refs[-1]
    for slot, ((k, ra), out) in enumerate(zip(jobs, outs)):
        spread_half(k, ra, metas[k], zz_ref, ww_ref, picked.at[slot % 2], out)


def spread(jobs, metas, zz, ww):
    ks = sorted({k for k, _ in jobs})
    half = jax.ShapeDtypeStruct((B, NO * B), F32)
    return pl.pallas_call(
        functools.partial(spread_kernel, jobs),
        out_shape=(half,) * len(jobs),
        in_specs=smem(len(ks)) + vmem(2),
        out_specs=tuple(vmem(len(jobs))),
        scratch_shapes=[pltpu.VMEM((2, NO * B, 4 * B), BF16)],
        compiler_params=PARAMS,
        name="spread",
    )(*(metas[k] for k in ks), zz, ww)


def finish_kernel(ds, *refs):
    n = len(ds)
    metas, xs = dict(zip(ds, refs)), refs[n : 2 * n]
    hh_ref, hl_ref, zz_ref, w_in, ww_ref, p5, p41, p40, w_ref, picked = refs[2 * n :]
    w_ref[...] = w_in[...]
    for d, x_ref in zip(ds, xs):
        add_rows(d, metas[d], x_ref, hh_ref, hl_ref, w_ref)
    for f in range(NC):
        hi, lo = split(w_ref[f])
        ww_ref[f, :, 0 : 2 * B] = hi
        ww_ref[f, :, 2 * B :] = lo
    spread_half(5, 0, metas[5], zz_ref, ww_ref, picked.at[0], p5.at[0:B])
    spread_half(5, 1, metas[5], zz_ref, ww_ref, picked.at[1], p5.at[B : 2 * B])
    spread_half(4, 1, metas[4], zz_ref, ww_ref, picked.at[0], p41)
    spread_half(4, 0, metas[4], zz_ref, ww_ref, picked.at[1], p40)


def finish(ds, metas, xs, hh, hl, zz, w):
    half = jax.ShapeDtypeStruct((B, NO * B), F32)
    return pl.pallas_call(
        functools.partial(finish_kernel, ds),
        out_shape=(
            jax.ShapeDtypeStruct((NC, B, 4 * B), BF16),
            jax.ShapeDtypeStruct((2 * B, NO * B), F32),
            half,
            half,
        ),
        in_specs=smem(len(ds)) + vmem(len(ds) + 4),
        out_specs=tuple(vmem(4)),
        scratch_shapes=[
            pltpu.VMEM((NC, B, 2 * B), F32),
            pltpu.VMEM((2, NO * B, 4 * B), BF16),
        ],
        compiler_params=PARAMS,
        name="finish",
    )(*(metas[d] for d in ds), *xs, hh, hl, zz, w)


def unpack_kernel(*refs):
    out_ref = refs[-1]
    for ra in range(2):
        total = refs[3 * ra][...] + refs[3 * ra + 1][...] + refs[3 * ra + 2][...]
        for o in range(NO):
            out_ref[ra, o] = total[:, o * B : (o + 1) * B]


def unpack(*parts):
    return pl.pallas_call(
        unpack_kernel,
        out_shape=jax.ShapeDtypeStruct((2, NO, B, B), F32),
        in_specs=vmem(6),
        out_specs=pl.BlockSpec(memory_space=pltpu.VMEM),
        compiler_params=PARAMS,
        name="unpack",
    )(*parts)


def local(h_blocks, h_cols, z_blocks, z_cols, out_cols):
    here = jnp.stack([lax.axis_index(AXES) * 2, jnp.int32(2 * lax.axis_size(AXES))])
    cols = jnp.concatenate([h_cols, z_cols, out_cols], axis=1)
    own, h_off, meta = pack(here, cols, z_blocks.reshape(NZ, 2 * B, B))
    up = {0: own}
    down = {0: own}
    for d in range(1, REACH):
        up[d] = shift(up[d - 1], -1)
        down[d] = shift(down[d - 1], 1)
    metas = {0: meta}
    down[REACH] = shift(up[8 - REACH], 8)
    far = jnp.concatenate(
        [down[8 - REACH][0 : ZROWS + 4], down[8 - LAST][ZROWS : ZROWS + 4]], axis=0
    )
    up[REACH] = shift(far, -8)

    def note(d):
        metas[d] = up[d][ZROWS:].astype(jnp.int32)
        metas[-d] = down[d][ZROWS:].astype(jnp.int32)

    for d in range(1, REACH + 1):
        note(d)
    metas[LAST] = up[REACH][ZROWS + 4 :].astype(jnp.int32)
    hh, hl, zz = prep(h_off, meta, h_blocks, z_blocks)

    def step(ds, w):
        xs = [up[d] if d >= 0 else down[-d] for d in ds]
        return gather(ds, [metas[d] for d in ds], xs, hh, hl, w)

    w = step((0,), None)
    w = step((1, -1), w)
    w = step((2, -2), w)
    w = step((3, -3), w)
    ww, p5, p41, p40 = finish(
        (-5, 5, -4, 4),
        metas,
        [up[d] if d >= 0 else down[-d] for d in (-5, 5, -4, 4)],
        hh,
        hl,
        zz,
        w,
    )

    def parts(*jobs):
        return spread(jobs, metas, zz, ww)

    back = shift(p5, -1)
    ahead1 = shift(p41, 1)
    ahead0 = shift(p40, 1)
    p31, p30, p60, p61, p21, p20, p11, p10, p00, p01 = parts(
        (3, 1), (3, 0), (6, 0), (6, 1), (2, 1), (2, 0), (1, 1), (1, 0), (0, 0), (0, 1)
    )
    ahead1 = shift(ahead1 + p31, 1)
    ahead0 = shift(ahead0 + p30, 1)
    back = shift(back + jnp.concatenate([p60, p61], axis=0), LAST)
    ahead1 = shift(ahead1 + p21, 1)
    ahead0 = shift(ahead0 + p20, 1)
    ahead1 = shift(ahead1 + p11, 1)
    ahead0 = shift(ahead0 + p10, 1)
    back0, back1 = back[0:B], back[B:]
    return unpack(p00, ahead0, back0, p01, ahead1, back1)


def solution(mesh):
    rows = P(AXES, None)
    blocks = P(AXES, None, None, None)
    return jax.shard_map(
        local,
        mesh=mesh,
        in_specs=(blocks, rows, blocks, rows, rows),
        out_specs=blocks,
        check_vma=False,
    )
```

```python
import functools

import jax
import jax.numpy as jnp
from jax import lax
from jax.experimental import pallas as pl
from jax.experimental.pallas import tpu as pltpu
from jax.sharding import PartitionSpec as P

NH = 20
NZ = 12
NO = 16
HS = 10
ZS = 13
B = 64
AXES = ("row", "col", "layer")
REACH = 5
LAST = 6
NJ = 2 * (2 * REACH + 1)
NC = NJ + ZS - 1
NA = 2 * (LAST + 1)
HALF = NZ // 2 * B
ZROWS = 2 * HALF
F32 = jnp.float32
BF16 = jnp.bfloat16

PARAMS = pltpu.CompilerParams(vmem_limit_bytes=48 * 1024 * 1024)


def split(x):
    hi = x.astype(BF16)
    return hi, (x - hi.astype(F32)).astype(BF16)


def shift(x, by):
    size = lax.axis_size(AXES)
    return lax.ppermute(x, AXES, [(i, (i + by) % size) for i in range(size)])


def vmem(count):
    return [pl.BlockSpec(memory_space=pltpu.VMEM)] * count


def smem(count):
    return [pl.BlockSpec(memory_space=pltpu.SMEM)] * count


def pack_kernel(here_ref, cols, z_ref, out_ref, h_off, meta_ref):
    total = here_ref[1]

    def offsets(at, count, low):
        rows = lax.broadcasted_iota(jnp.int32, (2, count), 0) + here_ref[0]
        away = cols[:, at : at + count] - rows
        away = jnp.where(away < low, away + total, away)
        return jnp.where(away >= low + total, away - total, away)

    h_off[...] = offsets(0, NH, -HS)
    meta_ref[...] = jnp.zeros_like(meta_ref)
    meta_ref[0:2, 0:NZ] = offsets(NH, NZ, 0)
    meta_ref[2:4, 0:NO] = offsets(NH + NZ, NO, -HS) + HS
    out_ref[ZROWS:, :] = meta_ref[...].astype(F32)
    for t in range(NZ):
        out_ref[t * B : (t + 1) * B, :] = z_ref[t].T


def pack(here, cols, z_pairs):
    return pl.pallas_call(
        pack_kernel,
        out_shape=(
            jax.ShapeDtypeStruct((ZROWS + 8, 2 * B), F32),
            jax.ShapeDtypeStruct((2, NH), jnp.int32),
            jax.ShapeDtypeStruct((8, 2 * B), jnp.int32),
        ),
        in_specs=smem(1) + vmem(2),
        out_specs=tuple(vmem(3)),
        compiler_params=PARAMS,
        name="pack",
    )(here, cols, z_pairs)


def prep_kernel(h_off, meta, h_ref, z_ref, hh_ref, hl_ref, zz_ref, stack):
    stack[...] = jnp.zeros_like(stack)
    for r in range(2):
        for k in range(NH):
            stack[h_off[r, k] + (HS + r), r * B : (r + 1) * B, :] = h_ref[r, k]
    for e in range(NJ):
        hi, lo = split(stack[e].T)
        hh_ref[e] = hi
        hl_ref[e] = lo
    stack[0:NA] = jnp.zeros((NA,) + stack.shape[1:], F32)
    for r in range(2):
        for m in range(NZ):
            stack[meta[r, m] + r, r * B : (r + 1) * B, :] = z_ref[r, m]
    for a in range(NA):
        hi, lo = split(stack[a].T)
        zz_ref[a, 0:B, 0 : 2 * B] = hi
        zz_ref[a, 0:B, 2 * B :] = hi
        zz_ref[a, B:, 0 : 2 * B] = lo
        zz_ref[a, B:, 2 * B :] = jnp.zeros_like(lo)


def prep(h_off, meta, h_blocks, z_blocks):
    return pl.pallas_call(
        prep_kernel,
        out_shape=(
            jax.ShapeDtypeStruct((NJ, B, 2 * B), BF16),
            jax.ShapeDtypeStruct((NJ, B, 2 * B), BF16),
            jax.ShapeDtypeStruct((NA, 2 * B, 4 * B), BF16),
        ),
        in_specs=smem(2) + vmem(2),
        out_specs=tuple(vmem(3)),
        scratch_shapes=[pltpu.VMEM((NJ, 2 * B, B), F32)],
        compiler_params=PARAMS,
        name="prep",
    )(h_off, meta, h_blocks, z_blocks)


def add_rows(d, meta, x_ref, hh_ref, hl_ref, w_ref):
    for r in range(2):
        e = 2 * (d + REACH) + r
        hi, lo = split(x_ref[r * HALF : (r + 1) * HALF, :])
        hh, hl = hh_ref[e], hl_ref[e]
        none = jnp.zeros_like(hh)
        top = jnp.concatenate([hh, none], axis=1)
        low = jnp.concatenate([none, hh], axis=1)
        main = jnp.concatenate([top, low, top, low], axis=0)
        rest = jnp.concatenate(
            [jnp.concatenate([hl, none], axis=1), jnp.concatenate([none, hl], axis=1)], axis=0
        )
        products = jnp.dot(
            jnp.concatenate([hi, lo], axis=1), main, preferred_element_type=F32
        ) + jnp.dot(hi, rest, preferred_element_type=F32)
        for m in range(NZ):
            at = meta[r, m] + e
            part = products[m // 2 * B : (m // 2 + 1) * B, m % 2 * 2 * B : (m % 2 + 1) * 2 * B]
            w_ref[at] = w_ref[at] + part


def gather_kernel(ds, first, *refs):
    n = len(ds)
    metas, xs = refs[:n], refs[n : 2 * n]
    hh_ref, hl_ref, w_ref = refs[2 * n], refs[2 * n + 1], refs[-1]
    w_ref[...] = jnp.zeros_like(w_ref) if first else refs[-2][...]
    for d, meta, x_ref in zip(ds, metas, xs):
        add_rows(d, meta, x_ref, hh_ref, hl_ref, w_ref)


def gather(ds, metas, xs, hh, hl, w):
    n = len(ds)
    first = w is None
    return pl.pallas_call(
        functools.partial(gather_kernel, ds, first),
        out_shape=jax.ShapeDtypeStruct((NC, B, 2 * B), F32),
        in_specs=smem(n) + vmem(n + 2 + (not first)),
        out_specs=pl.BlockSpec(memory_space=pltpu.VMEM),
        compiler_params=PARAMS,
        name="gather",
    )(*metas, *xs, hh, hl, *([] if first else [w]))


def spread_half(k, ra, meta, zz_ref, ww_ref, picked, out):
    a = 2 * k + ra
    for o in range(NO):
        picked[o * B : (o + 1) * B, :] = ww_ref[meta[2 + ra, o] + a]
    both = lax.dot_general(
        zz_ref[a], picked[...], (((1,), (1,)), ((), ())), preferred_element_type=F32
    )
    out[...] = both[0:B] + both[B:]


def spread_kernel(jobs, *refs):
    ks = sorted({k for k, _ in jobs})
    metas = dict(zip(ks, refs))
    zz_ref, ww_ref = refs[len(ks) : len(ks) + 2]
    outs, picked = refs[len(ks) + 2 : -1], refs[-1]
    for slot, ((k, ra), out) in enumerate(zip(jobs, outs)):
        spread_half(k, ra, metas[k], zz_ref, ww_ref, picked.at[slot % 2], out)


def spread(jobs, metas, zz, ww):
    ks = sorted({k for k, _ in jobs})
    half = jax.ShapeDtypeStruct((B, NO * B), F32)
    return pl.pallas_call(
        functools.partial(spread_kernel, jobs),
        out_shape=(half,) * len(jobs),
        in_specs=smem(len(ks)) + vmem(2),
        out_specs=tuple(vmem(len(jobs))),
        scratch_shapes=[pltpu.VMEM((2, NO * B, 4 * B), BF16)],
        compiler_params=PARAMS,
        name="spread",
    )(*(metas[k] for k in ks), zz, ww)


def finish_kernel(ds, *refs):
    n = len(ds)
    metas, xs = dict(zip(ds, refs)), refs[n : 2 * n]
    hh_ref, hl_ref, zz_ref, w_in, ww_ref, p5, p41, p40, w_ref, picked = refs[2 * n :]
    w_ref[...] = jnp.zeros_like(w_ref)
    for d, x_ref in zip(ds, xs):
        add_rows(d, metas[d], x_ref, hh_ref, hl_ref, w_ref)
    for f in range(NC):
        hi, lo = split(w_in[f] + w_ref[f])
        ww_ref[f, :, 0 : 2 * B] = hi
        ww_ref[f, :, 2 * B :] = lo
    spread_half(5, 0, metas[5], zz_ref, ww_ref, picked.at[0], p5.at[0:B])
    spread_half(5, 1, metas[5], zz_ref, ww_ref, picked.at[1], p5.at[B : 2 * B])
    spread_half(4, 1, metas[4], zz_ref, ww_ref, picked.at[0], p41)
    spread_half(4, 0, metas[4], zz_ref, ww_ref, picked.at[1], p40)


def finish(ds, metas, xs, hh, hl, zz, w):
    half = jax.ShapeDtypeStruct((B, NO * B), F32)
    return pl.pallas_call(
        functools.partial(finish_kernel, ds),
        out_shape=(
            jax.ShapeDtypeStruct((NC, B, 4 * B), BF16),
            jax.ShapeDtypeStruct((2 * B, NO * B), F32),
            half,
            half,
        ),
        in_specs=smem(len(ds)) + vmem(len(ds) + 4),
        out_specs=tuple(vmem(4)),
        scratch_shapes=[
            pltpu.VMEM((NC, B, 2 * B), F32),
            pltpu.VMEM((2, NO * B, 4 * B), BF16),
        ],
        compiler_params=PARAMS,
        name="finish",
    )(*(metas[d] for d in ds), *xs, hh, hl, zz, w)


def unpack_kernel(*refs):
    out_ref = refs[-1]
    for ra in range(2):
        total = refs[3 * ra][...] + refs[3 * ra + 1][...] + refs[3 * ra + 2][...]
        for o in range(NO):
            out_ref[ra, o] = total[:, o * B : (o + 1) * B]


def unpack(*parts):
    return pl.pallas_call(
        unpack_kernel,
        out_shape=jax.ShapeDtypeStruct((2, NO, B, B), F32),
        in_specs=vmem(6),
        out_specs=pl.BlockSpec(memory_space=pltpu.VMEM),
        compiler_params=PARAMS,
        name="unpack",
    )(*parts)


def local(h_blocks, h_cols, z_blocks, z_cols, out_cols):
    here = jnp.stack([lax.axis_index(AXES) * 2, jnp.int32(2 * lax.axis_size(AXES))])
    cols = jnp.concatenate([h_cols, z_cols, out_cols], axis=1)
    own, h_off, meta = pack(here, cols, z_blocks.reshape(NZ, 2 * B, B))
    up = {0: own}
    down = {0: own}
    for d in range(1, REACH):
        up[d] = shift(up[d - 1], -1)
        down[d] = shift(down[d - 1], 1)
    metas = {0: meta}
    down[REACH] = shift(up[8 - REACH], 8)
    far = jnp.concatenate(
        [down[8 - REACH][0 : ZROWS + 4], down[8 - LAST][ZROWS : ZROWS + 4]], axis=0
    )
    up[REACH] = shift(far, -8)

    def note(d):
        metas[d] = up[d][ZROWS:].astype(jnp.int32)
        metas[-d] = down[d][ZROWS:].astype(jnp.int32)

    for d in range(1, REACH + 1):
        note(d)
    metas[LAST] = up[REACH][ZROWS + 4 :].astype(jnp.int32)
    hh, hl, zz = prep(h_off, meta, h_blocks, z_blocks)

    def step(ds, w):
        xs = [up[d] if d >= 0 else down[-d] for d in ds]
        return gather(ds, [metas[d] for d in ds], xs, hh, hl, w)

    w = step((0,), None)
    w = step((1, -1), w)
    w = step((2, -2), w)
    w = step((3, -3), w)
    ww, p5, p41, p40 = finish(
        (-5, 5, -4, 4),
        metas,
        [up[d] if d >= 0 else down[-d] for d in (-5, 5, -4, 4)],
        hh,
        hl,
        zz,
        w,
    )

    def parts(*jobs):
        return spread(jobs, metas, zz, ww)

    back = shift(p5, -1)
    ahead1 = shift(p41, 1)
    ahead0 = shift(p40, 1)
    p31, p30, p60, p61, p21, p20, p11, p10, p00, p01 = parts(
        (3, 1), (3, 0), (6, 0), (6, 1), (2, 1), (2, 0), (1, 1), (1, 0), (0, 0), (0, 1)
    )
    ahead1 = shift(ahead1 + p31, 1)
    ahead0 = shift(ahead0 + p30, 1)
    back = shift(back + jnp.concatenate([p60, p61], axis=0), LAST)
    ahead1 = shift(ahead1 + p21, 1)
    ahead0 = shift(ahead0 + p20, 1)
    ahead1 = shift(ahead1 + p11, 1)
    ahead0 = shift(ahead0 + p10, 1)
    back0, back1 = back[0:B], back[B:]
    return unpack(p00, ahead0, back0, p01, ahead1, back1)


def solution(mesh):
    rows = P(AXES, None)
    blocks = P(AXES, None, None, None)
    return jax.shard_map(
        local,
        mesh=mesh,
        in_specs=(blocks, rows, blocks, rows, rows),
        out_specs=blocks,
        check_vma=False,
    )
```
